32 devices in a mesh: layer: 8 (over y, x, core), row: 4 (over z).
Axes of the slice: x: 2, y: 2, z: 4, core: 2. Of those that a mesh axis runs over, the one named last changes fastest.
Arguments:
- green: bfloat16 [8, 8192, 8192], P('layer', 'row'), may hold values from -0.09375 to 0.09375
- source_traces: bfloat16 [8, 128, 8192], P('layer', None, 'row'), may hold values from -6 to 6
Outputs:
- traces: bfloat16 [8, 128, 8192], P('layer', None, 'row')
The draws below stay inside these ranges and needn't reach their ends.
All inputs are finite; a program needn't handle non-finite values.
Results may differ from the reference program's by a relative error of at most 0.007.
Values may be sent and summed in bfloat16 or wider, within the bound.
A program may use at most 128 MiB of HBM per device.

```python
import jax
import jax.numpy as jnp
from jax import lax

M = 8192
S = 64
ITERS = 4
LAYERS = 8


def spiked(array, key, source, target, shards_of, factor):
    def block_of(position):
        return (jnp.arange(array.shape[position]) // (array.shape[position] // shards_of)).reshape((-1,) + (1,) * (array.ndim - 1 - position))

    near = jax.random.permutation(key, shards_of)[block_of(target)]
    second = (block_of(target) + shards_of // 2) % shards_of
    return jnp.where((block_of(source) == near) | (block_of(source) == second), factor * array, array)


def block_levels(key, dims, pieces, low, top_value):
    level = 1.0
    for position, parts in pieces:
        steps = jax.random.uniform(jax.random.fold_in(jax.random.fold_in(key, 6), position), (parts,), jnp.float32, low / len(pieces), top_value / len(pieces))
        level = level * jnp.repeat(jnp.exp(steps), dims[position] // parts).reshape((-1,) + (1,) * (len(dims) - 1 - position))
    return level


def normal_values(rng, dims, width, limit, cuts=(), held_as=jnp.bfloat16):
    loudness = block_levels(rng, dims, cuts, -0.22, 0.18) if cuts else 1.0
    entries = jax.random.normal(rng, dims, jnp.float32) * width * loudness
    return jnp.minimum(jnp.maximum(entries, -limit), limit).astype(held_as)


def bell_draw_with(stream_key, shape, scale, most, shards, heavy, dtype=jnp.bfloat16):
    drawn = scale * jax.random.normal(stream_key, shape, jnp.float32)
    if shards:
        drawn = drawn * block_levels(stream_key, shape, shards, -0.22, 0.18)
    return jnp.clip(spiked(drawn, jax.random.fold_in(stream_key, 3), *heavy), -most, most).astype(dtype)


def setup_inputs(seed: int = 0) -> dict:
    splits = jax.random.split(jax.random.key(seed), 3)
    return {
        "green": bell_draw_with(splits[0], (LAYERS, M, M), M ** -0.5, 0.09375, ((0, 8), (1, 4)), (1, 2, 4, 2.0)),
        "source_traces": normal_values(splits[1], (LAYERS, 2 * S, M), 1.0, 6.0, ((0, 8), (2, 4))),
    }


def apply_layer(pair):
    incoming, matrix = pair
    return jnp.dot(incoming, matrix, preferred_element_type=jnp.float32)


def reference(green, source_traces):
    traces = source_traces
    half = source_traces.shape[1] // 2
    for step in range(ITERS):
        zero_block = jnp.zeros((1, half, M), jnp.bfloat16)
        down_in = jnp.concatenate([zero_block, traces[:-1, :half]], axis=0)
        up_in = jnp.concatenate([traces[1:, half:], zero_block], axis=0)
        incoming = jnp.concatenate([down_in, up_in], axis=1)
        applied = lax.map(apply_layer, (incoming, green))
        traces = (source_traces.astype(jnp.float32) + applied).astype(jnp.bfloat16)
    return traces
```

```python
import functools

import jax
import jax.numpy as jnp
from jax import lax
from jax.experimental import pallas as pl
from jax.experimental.pallas import tpu as pltpu
from jax.sharding import PartitionSpec as P

ITERS = 4
MESH = pl.DeviceIdType.MESH


def block_order(z, i, R):
    flip = (2 * z) // R
    zz = flip * (R - 1 - z) + (1 - flip) * z
    lead = R - 1 - 2 * zz
    tail = (i - lead + R) // R
    j2 = i - lead + 2 * R
    odd = j2 % 2
    h = j2 // 2 - R
    c = (1 - tail) * (R - 1 - i) + tail * ((1 - odd) * (2 * zz - h) + odd * h)
    return flip * (R - 1 - c) + (1 - flip) * c


def kernel(L, R, NC, green, src, out, g, inc, tr, rx, tx, acc,
           g_sem, inc_send, inc_recv, tx_sem, rx_sem):
    T = ITERS
    K = src.shape[2]
    H = src.shape[1] // 2
    KC = K // NC
    l = lax.axis_index("layer")
    z = lax.axis_index("row")
    span = max(L - 1 - T, 0)

    def place(half, layer):
        return layer if half == 0 else L - 1 - layer

    def active(half, t, layer):
        p = place(half, layer) - t
        return jnp.logical_and(p >= 0, p <= span)

    def sends_on(half, t):
        if t == T:
            return None
        p = place(half, l)
        return jnp.logical_and(p + 1 < L, jnp.logical_and(p - t >= 0, p - t <= span))

    def rows(half):
        return pl.ds(half * H, H)

    def cols(n):
        if isinstance(n, int):
            return pl.ds(n * KC, KC)
        return pl.ds(pl.multiple_of(n * KC, KC), KC)

    def green_copy(c, n):
        return pltpu.make_async_copy(
            green.at[0, :, pl.ds(pl.multiple_of(c * K + n * KC, KC), KC)],
            g.at[c, n], g_sem.at[c, n])

    def layer_copy(half, t, n):
        step = 1 if half == 0 else -1
        source = src.at[0] if t == 0 else tr.at[t - 1]
        return pltpu.make_async_remote_copy(
            src_ref=source.at[rows(half), cols(n)],
            dst_ref=inc.at[t, rows(half), cols(n)],
            send_sem=inc_send.at[t, half, n], recv_sem=inc_recv.at[t, half, n],
            device_id={"layer": l + step}, device_id_type=MESH)

    def row_copy(t, c, half, n, slot, to):
        return pltpu.make_async_remote_copy(
            src_ref=tx.at[c, half, n], dst_ref=rx.at[t - 1, slot, half, n],
            send_sem=tx_sem.at[c, half, n], recv_sem=rx_sem.at[t - 1, slot, half, n],
            device_id={"row": to}, device_id_type=MESH)

    def start_green(q, carry):
        green_copy(block_order(z, q // NC, R), q % NC).start()
        return carry

    lax.fori_loop(0, R * NC, start_green, 0)

    barrier = pltpu.get_barrier_semaphore()
    near = [(z > 0, {"row": z - 1}), (z < R - 1, {"row": z + 1}),
            (l > 0, {"layer": l - 1}), (l < L - 1, {"layer": l + 1})]
    for there, who in near:
        @pl.when(there)
        def _():
            pl.semaphore_signal(barrier, inc=1, device_id=who, device_id_type=MESH)
    peers = sum((at + size - 1) // size + (2 * size - 2 - at) // size
                for at, size in ((z, R), (l, L)))
    pl.semaphore_wait(barrier, peers)

    for half in range(2):
        @pl.when(sends_on(half, 0))
        def _():
            for n in range(NC):
                layer_copy(half, 0, n).start()

    for half in range(2):
        @pl.when(place(half, l) == 0)
        def _():
            out[0, rows(half), :] = src[0, rows(half), :]

    for t in range(1, T + 1):
        on = [active(half, t, l) for half in range(2)]
        either = jnp.logical_or(on[0], on[1])

        for half in range(2):
            @pl.when(on[half])
            def _():
                for n in range(NC):
                    layer_copy(half, t - 1, n).wait_recv()

            @pl.when(jnp.logical_and(either, jnp.logical_not(on[half])))
            def _():
                inc[t - 1, rows(half), :] = jnp.zeros((H, K), inc.dtype)

        def body(q, carry):
            i = q // NC
            n = q % NC
            c = block_order(z, i, R)
            if t == 1:
                green_copy(c, n).wait()

            @pl.when(either)
            def _():
                acc[...] = jnp.dot(inc[t - 1], g[c, n], preferred_element_type=jnp.float32)

            def add_received(half, slot):
                row_copy(t, c, half, n, slot, z).wait_recv()
                acc[rows(half), :] += rx[t - 1, slot, half, n].astype(jnp.float32)

            for half in range(2):
                @pl.when(jnp.logical_and(on[half], c != z))
                def _():
                    @pl.when(jnp.logical_or(jnp.logical_and(c > z, z > 0),
                                            jnp.logical_and(c < z, z < R - 1)))
                    def _():
                        add_received(half, c)

                    if t > 1:
                        @pl.when(active(half, t - 1, l))
                        def _():
                            row_copy(t, c, half, n, c, z).wait_send()

                    tx[c, half, n] = acc[rows(half), :].astype(tx.dtype)

                    @pl.when(c > z)
                    def _():
                        row_copy(t, c, half, n, c, z + 1).start()

                    @pl.when(c < z)
                    def _():
                        last = (c + 1 - z + R) // R
                        row_copy(t, c, half, n, c + last * (R - c), z - 1).start()

                @pl.when(jnp.logical_and(on[half], c == z))
                def _():
                    @pl.when(z > 0)
                    def _():
                        add_received(half, z)

                    @pl.when(z < R - 1)
                    def _():
                        add_received(half, R)

                    new = (src[0, rows(half), cols(n)].astype(jnp.float32)
                           + acc[rows(half), :]).astype(tr.dtype)

                    @pl.when(place(half, l) >= t if t == T else place(half, l) == t)
                    def _():
                        out[0, rows(half), cols(n)] = new

                    if t < T:
                        tr[t - 1, rows(half), cols(n)] = new

                        @pl.when(sends_on(half, t))
                        def _():
                            layer_copy(half, t, n).start()
            return carry

        lax.fori_loop(0, R * NC, body, 0)

    for half in range(2):
        for t in range(T):
            @pl.when(sends_on(half, t))
            def _():
                for n in range(NC):
                    layer_copy(half, t, n).wait_send()

        @pl.when(place(half, l) > 0)
        def _():
            def drain(q, carry):
                c = q // NC

                @pl.when(c != z)
                def _():
                    row_copy(1, c, half, q % NC, c, z).wait_send()
                return carry

            lax.fori_loop(0, R * NC, drain, 0)


def solution(mesh):
    L, R = mesh.shape["layer"], mesh.shape["row"]
    T = ITERS

    def local(green, source_traces):
        _, H2, K = source_traces.shape
        H = H2 // 2
        M = green.shape[2]
        KC = min(512, K)
        NC = K // KC
        bf = jnp.bfloat16
        dma = pltpu.SemaphoreType.DMA
        return pl.pallas_call(
            functools.partial(kernel, L, R, NC),
            out_shape=jax.ShapeDtypeStruct(source_traces.shape, bf),
            in_specs=[pl.BlockSpec(memory_space=pl.ANY),
                      pl.BlockSpec(memory_space=pltpu.VMEM)],
            out_specs=pl.BlockSpec(memory_space=pltpu.VMEM),
            scratch_shapes=[
                pltpu.VMEM((R, NC, K, KC), bf),
                pltpu.VMEM((T, H2, K), bf),
                pltpu.VMEM((T - 1, H2, K), bf),
                pltpu.VMEM((T, R + 1, 2, NC, H, KC), bf),
                pltpu.VMEM((R, 2, NC, H, KC), bf),
                pltpu.VMEM((H2, KC), jnp.float32),
                dma((R, NC)),
                dma((T, 2, NC)),
                dma((T, 2, NC)),
                dma((R, 2, NC)),
                dma((T, R + 1, 2, NC)),
            ],
            compiler_params=pltpu.CompilerParams(
                collective_id=0, has_side_effects=True,
                vmem_limit_bytes=60 * 2**20),
            cost_estimate=pl.CostEstimate(
                flops=2 * T * H2 * K * M, bytes_accessed=2 * K * M, transcendentals=0),
        )(green, source_traces)

    return jax.shard_map(
        local,
        mesh=mesh,
        in_specs=(P("layer", "row", None), P("layer", None, "row")),
        out_specs=P("layer", None, "row"),
        check_vma=False,
    )
```

```python
import functools

import jax
import jax.numpy as jnp
from jax import lax
from jax.experimental import pallas as pl
from jax.experimental.pallas import tpu as pltpu
from jax.sharding import PartitionSpec as P

ITERS = 4
MESH = pl.DeviceIdType.MESH


def block_order(z, i, R):
    flip = (2 * z) // R
    zz = flip * (R - 1 - z) + (1 - flip) * z
    lead = R - 1 - 2 * zz
    tail = (i - lead + R) // R
    j2 = i - lead + 2 * R
    odd = j2 % 2
    h = j2 // 2 - R
    c = (1 - tail) * (R - 1 - i) + tail * ((1 - odd) * (2 * zz - h) + odd * h)
    return flip * (R - 1 - c) + (1 - flip) * c


def below(a, k, n):
    return 1 - (a - k + n) // n


def equal(a, k, n):
    return below(a, k + 1, n) - below(a, k, n)


def kernel(L, R, NC, green, src, out, g, inc, tr, rx, tx, acc, ry,
           g_sem, inc_send, inc_recv, tx_sem, rx_sem, ry_send, ry_recv):
    T = ITERS
    K = src.shape[2]
    H = src.shape[1] // 2
    KC = K // NC
    l = lax.axis_index("layer")
    z = lax.axis_index("row")
    span = max(L - 1 - T, 0)

    def place(half, layer):
        return layer if half == 0 else L - 1 - layer

    def active(half, t, layer):
        p = place(half, layer) - t
        return jnp.logical_and(p >= 0, p <= span)

    def sends_on(half, t):
        if t == T:
            return None
        p = place(half, l)
        return jnp.logical_and(p + 1 < L, jnp.logical_and(p - t >= 0, p - t <= span))

    relayed = L % 4 == 0 and L >= 8 and R >= 3
    turn = (2 * l) // L
    depth = turn * (L - 1 - l) + (1 - turn) * l
    helper = below(depth, 2, L)
    helped = below(depth, 4, L) - helper
    mate = l + 2 - 4 * ((l // 2) % 2)
    ends = ((0, 1), (R - 1, R - 2)) if relayed else ()

    def rows(half):
        return pl.ds(half * H, H)

    def cols(n):
        if isinstance(n, int):
            return pl.ds(n * KC, KC)
        return pl.ds(pl.multiple_of(n * KC, KC), KC)

    def green_copy(c, n):
        return pltpu.make_async_copy(
            green.at[0, :, pl.ds(pl.multiple_of(c * K + n * KC, KC), KC)],
            g.at[c, n], g_sem.at[c, n])

    def layer_copy(half, t, n):
        step = 1 if half == 0 else -1
        source = src.at[0] if t == 0 else tr.at[t - 1]
        return pltpu.make_async_remote_copy(
            src_ref=source.at[rows(half), cols(n)],
            dst_ref=inc.at[t, rows(half), cols(n)],
            send_sem=inc_send.at[t, half, n], recv_sem=inc_recv.at[t, half, n],
            device_id={"layer": l + step}, device_id_type=MESH)

    def row_copy(t, c, half, n, slot, to):
        return pltpu.make_async_remote_copy(
            src_ref=tx.at[c, half, n], dst_ref=rx.at[t - 1, slot, half, n],
            send_sem=tx_sem.at[c, half, n], recv_sem=rx_sem.at[t - 1, slot, half, n],
            device_id={"row": to}, device_id_type=MESH)

    def to_relay(t, c, half, n):
        return pltpu.make_async_remote_copy(
            src_ref=tx.at[c, half, n], dst_ref=ry.at[t - 1, half, n],
            send_sem=tx_sem.at[c, half, n], recv_sem=ry_recv.at[t - 1, half, n],
            device_id={"layer": mate}, device_id_type=MESH)

    def from_relay(t, half, n, slot, to):
        return pltpu.make_async_remote_copy(
            src_ref=ry.at[t - 1, half, n], dst_ref=rx.at[t - 1, slot, half, n],
            send_sem=ry_send.at[t - 1, half, n], recv_sem=rx_sem.at[t - 1, slot, half, n],
            device_id={"layer": mate, "row": to}, device_id_type=MESH)

    def relays(half, t):
        return jnp.logical_and(helper == 1, active(half, t, mate))

    def start_green(q, carry):
        green_copy(block_order(z, q // NC, R), q % NC).start()
        return carry

    lax.fori_loop(0, R * NC, start_green, 0)

    barrier = pltpu.get_barrier_semaphore()
    near = [(z > 0, {"row": z - 1}), (z < R - 1, {"row": z + 1}),
            (l > 0, {"layer": l - 1}), (l < L - 1, {"layer": l + 1})]
    peers = sum((at + size - 1) // size + (2 * size - 2 - at) // size
                for at, size in ((z, R), (l, L)))
    for end, beside in ends:
        near += [(jnp.logical_and(helper + helped == 1, z == end), {"layer": mate}),
                 (jnp.logical_and(helper == 1, z == end), {"layer": mate, "row": beside}),
                 (jnp.logical_and(helped == 1, z == beside), {"layer": mate, "row": end})]
        peers += ((2 * helper + helped) * equal(z, end, R) + helped * equal(z, beside, R))
    for there, who in near:
        @pl.when(there)
        def _():
            pl.semaphore_signal(barrier, inc=1, device_id=who, device_id_type=MESH)
    pl.semaphore_wait(barrier, peers)

    for half in range(2):
        @pl.when(sends_on(half, 0))
        def _():
            for n in range(NC):
                layer_copy(half, 0, n).start()

    for half in range(2):
        @pl.when(place(half, l) == 0)
        def _():
            out[0, rows(half), :] = src[0, rows(half), :]

    for t in range(1, T + 1):
        on = [active(half, t, l) for half in range(2)]
        either = jnp.logical_or(on[0], on[1])

        for half in range(2):
            @pl.when(on[half])
            def _():
                for n in range(NC):
                    layer_copy(half, t - 1, n).wait_recv()

            @pl.when(jnp.logical_and(either, jnp.logical_not(on[half])))
            def _():
                inc[t - 1, rows(half), :] = jnp.zeros((H, K), inc.dtype)

        def body(q, carry):
            i = q // NC
            n = q % NC
            c = block_order(z, i, R)
            if t == 1:
                green_copy(c, n).wait()

            @pl.when(either)
            def _():
                acc[...] = jnp.dot(inc[t - 1], g[c, n], preferred_element_type=jnp.float32)

            if t < T:
                for end, beside in ends:
                    @pl.when(jnp.logical_and(q == (R - 1) * NC,
                                             jnp.logical_and(helper == 1, z == end)))
                    def _():
                        def hand_on(m, carry):
                            for half in range(2):
                                @pl.when(relays(half, t))
                                def _():
                                    to_relay(t, 0, half, m).wait_recv()
                                    from_relay(t, half, m, 1 if end == 0 else R, beside).start()
                            return carry

                        lax.fori_loop(0, NC, hand_on, 0)

            def add_received(half, slot):
                row_copy(t, c, half, n, slot, z).wait_recv()
                acc[rows(half), :] += rx[t - 1, slot, half, n].astype(jnp.float32)

            for half in range(2):
                @pl.when(jnp.logical_and(on[half], c != z))
                def _():
                    @pl.when(jnp.logical_or(jnp.logical_and(c > z, z > 0),
                                            jnp.logical_and(c < z, z < R - 1)))
                    def _():
                        add_received(half, c)

                    if t > 1:
                        @pl.when(active(half, t - 1, l))
                        def _():
                            row_copy(t, c, half, n, c, z).wait_send()

                    tx[c, half, n] = acc[rows(half), :].astype(tx.dtype)

                    aside = False
                    if t < T:
                        for end, beside in ends:
                            aside = jnp.logical_or(aside, jnp.logical_and(
                                helped == 1, jnp.logical_and(z == end, c == beside)))
                    straight = jnp.logical_not(aside)
                    if t < T and ends:
                        @pl.when(aside)
                        def _():
                            to_relay(t, c, half, n).start()

                    @pl.when(jnp.logical_and(straight, c > z))
                    def _():
                        row_copy(t, c, half, n, c, z + 1).start()

                    @pl.when(jnp.logical_and(straight, c < z))
                    def _():
                        last = (c + 1 - z + R) // R
                        row_copy(t, c, half, n, c + last * (R - c), z - 1).start()

                @pl.when(jnp.logical_and(on[half], c == z))
                def _():
                    @pl.when(z > 0)
                    def _():
                        add_received(half, z)

                    @pl.when(z < R - 1)
                    def _():
                        add_received(half, R)

                    new = (src[0, rows(half), cols(n)].astype(jnp.float32)
                           + acc[rows(half), :]).astype(tr.dtype)

                    @pl.when(place(half, l) >= t if t == T else place(half, l) == t)
                    def _():
                        out[0, rows(half), cols(n)] = new

                    if t < T:
                        tr[t - 1, rows(half), cols(n)] = new

                        @pl.when(sends_on(half, t))
                        def _():
                            layer_copy(half, t, n).start()
            return carry

        lax.fori_loop(0, R * NC, body, 0)

    for half in range(2):
        if ends:
            for t in range(1, T):
                @pl.when(jnp.logical_and(relays(half, t), jnp.logical_or(z == 0, z == R - 1)))
                def _():
                    for n in range(NC):
                        from_relay(t, half, n, 1, 1).wait_send()

        for t in range(T):
            @pl.when(sends_on(half, t))
            def _():
                for n in range(NC):
                    layer_copy(half, t, n).wait_send()

        @pl.when(place(half, l) > 0)
        def _():
            def drain(q, carry):
                c = q // NC

                @pl.when(c != z)
                def _():
                    row_copy(1, c, half, q % NC, c, z).wait_send()
                return carry

            lax.fori_loop(0, R * NC, drain, 0)


def solution(mesh):
    L, R = mesh.shape["layer"], mesh.shape["row"]
    T = ITERS

    def local(green, source_traces):
        _, H2, K = source_traces.shape
        H = H2 // 2
        M = green.shape[2]
        KC = min(512, K)
        NC = K // KC
        bf = jnp.bfloat16
        dma = pltpu.SemaphoreType.DMA
        return pl.pallas_call(
            functools.partial(kernel, L, R, NC),
            out_shape=jax.ShapeDtypeStruct(source_traces.shape, bf),
            in_specs=[pl.BlockSpec(memory_space=pl.ANY),
                      pl.BlockSpec(memory_space=pltpu.VMEM)],
            out_specs=pl.BlockSpec(memory_space=pltpu.VMEM),
            scratch_shapes=[
                pltpu.VMEM((R, NC, K, KC), bf),
                pltpu.VMEM((T, H2, K), bf),
                pltpu.VMEM((T - 1, H2, K), bf),
                pltpu.VMEM((T, R + 1, 2, NC, H, KC), bf),
                pltpu.VMEM((R, 2, NC, H, KC), bf),
                pltpu.VMEM((H2, KC), jnp.float32),
                pltpu.VMEM((T - 1, 2, NC, H, KC), bf),
                dma((R, NC)),
                dma((T, 2, NC)),
                dma((T, 2, NC)),
                dma((R, 2, NC)),
                dma((T, R + 1, 2, NC)),
                dma((T - 1, 2, NC)),
                dma((T - 1, 2, NC)),
            ],
            compiler_params=pltpu.CompilerParams(
                collective_id=0, has_side_effects=True,
                vmem_limit_bytes=60 * 2**20),
            cost_estimate=pl.CostEstimate(
                flops=2 * T * H2 * K * M, bytes_accessed=2 * K * M, transcendentals=0),
        )(green, source_traces)

    return jax.shard_map(
        local,
        mesh=mesh,
        in_specs=(P("layer", "row", None), P("layer", None, "row")),
        out_specs=P("layer", None, "row"),
        check_vma=False,
    )
```
